128 devices in a mesh: head: 4 (over z_hi, core), blk: 32 (over y, z_lo, x).
Axes of the slice: x: 4, y: 4, z: 4 (z_hi: 2, z_lo: 2; z = z_hi * 2 + z_lo), core: 2. Of those that a mesh axis runs over, the one named last changes fastest.
Arguments:
- inputs: bfloat16 [6144, 1, 3072], P('blk', None, 'head'), may hold values from -17.5 to 17.5
- out_grad: bfloat16 [6144, 1, 3072], P('blk', None, 'head'), may hold values from -6 to 6
- qkv_weight: bfloat16 [3072, 3, 1536], P(None, None, 'head'), may hold values from -0.108253175 to 0.108253175
- out_weight: bfloat16 [3072, 1536], P(None, 'head'), may hold values from -0.15625 to 0.15625
- text_keys: bfloat16 [256, 1, 1536], P(None, None, 'head'), may hold values from -6 to 6
- text_values: bfloat16 [256, 1, 1536], P(None, None, 'head'), may hold values from -6 to 6
- text_mask: int32 [256, 1], replicated, may hold values 0 or 1
Outputs:
- grad_inputs: bfloat16 [6144, 1, 3072], P('blk', None, 'head')
- grad_qkv_weight: float32 [3072, 3, 1536], P('blk', None, 'head')
- grad_out_weight: float32 [3072, 1536], P('blk', 'head')
- grad_text_keys: float32 [256, 1, 1536], P('blk', None, 'head')
- grad_text_values: float32 [256, 1, 1536], P('blk', None, 'head')
The draws below stay inside these ranges and needn't reach their ends.
All inputs are finite; a program needn't handle non-finite values.
Results may differ from the reference program's by a relative error of at most 0.034.
Values may be sent and summed in bfloat16 or wider, within the bound.
No kernel may reach another device: no remote copies, remote signals or barrier semaphores. Data moves between devices by JAX's collectives and lax.ppermute only.
A program may use at most 128 MiB of HBM per device.

```python
import jax
import jax.numpy as jnp
from jax import lax

D = 3072
HD = 128
TXT = 256
SEQS = 1
VID_DEV = 192
HEADS = 12
VIDEO = 6144
N_BLK = 32


def draw_inputs(key, part):
    key = jax.random.fold_in(key, 11)
    shape = (VIDEO, SEQS, D)
    values = jnp.clip(jax.random.normal(key, shape, jnp.float32), -6.0, 6.0)
    return values.astype(jnp.bfloat16)


def draw_qkv_weight(key, part):
    key = jax.random.fold_in(key, 31)
    shape = (D, 3, HEADS * HD)
    scale = D ** (-0.5)
    values = jnp.clip(jax.random.normal(key, shape, jnp.float32), -6.0, 6.0) * scale
    return values.astype(jnp.bfloat16)


def place_ends(drawn, key, least, high):
    longest = drawn.shape.index(max(drawn.shape))
    spots = []
    for shift in (0, 1):
        where = [jax.random.randint(jax.random.fold_in(key, axis), (), 0, length) for axis, length in enumerate(drawn.shape)]
        where[longest] = (where[longest] + shift) % drawn.shape[longest]
        spots.append(tuple(where))
    return drawn.at[spots[0]].set(least).at[spots[1]].set(high)


def strengthened(drawn, key, source, target, parts, factor):
    def block_of(dim):
        return (jnp.arange(drawn.shape[dim]) // (drawn.shape[dim] // parts)).reshape((-1,) + (1,) * (drawn.ndim - 1 - dim))

    one_side = jax.random.permutation(key, parts)[block_of(target)]
    second = (block_of(target) + parts // 2) % parts
    return jnp.where((block_of(source) == one_side) | (block_of(source) == second), factor * drawn, drawn)


def level_of(rng, extent, cuts, least, high):
    level = 1.0
    for dim, parts in cuts:
        steps = jax.random.uniform(jax.random.fold_in(jax.random.fold_in(rng, 6), dim), (parts,), jnp.float32, least / len(cuts), high / len(cuts))
        level = level * jnp.repeat(jnp.exp(steps), extent[dim] // parts).reshape((-1,) + (1,) * (len(extent) - 1 - dim))
    return level


def scatter_about(key, extent, deviation, reach, split=(), kind=jnp.bfloat16):
    factor_of = level_of(key, extent, split, -0.22, 0.18) if split else 1.0
    values = jax.random.normal(key, extent, jnp.float32) * deviation * factor_of
    return jnp.minimum(jnp.maximum(values, -reach), reach).astype(kind)


def noise_with(key, extent, scale, reach, cuts, heavy, kind=jnp.bfloat16):
    array = scale * jax.random.normal(key, extent, jnp.float32)
    if cuts:
        array = array * level_of(key, extent, cuts, -0.22, 0.18)
    return jnp.clip(strengthened(array, jax.random.fold_in(key, 3), *heavy), -reach, reach).astype(kind)


def setup_inputs(seed: int = 0) -> dict:
    splits = jax.random.split(jax.random.key(seed), 8)
    return {
        "inputs": draw_inputs(jax.random.fold_in(splits[7], 71), 0),
        "out_grad": noise_with(splits[1], (VIDEO, SEQS, D), 1.0, 6.0, ((0, 32), (2, 4)), (0, 2, 32, 2.75)),
        "qkv_weight": draw_qkv_weight(jax.random.fold_in(splits[7], 71), 0),
        "out_weight": scatter_about(splits[3], (D, HEADS * HD), (HEADS * HD) ** -0.5, 0.15625, ((1, 4),)),
        "text_keys": scatter_about(splits[4], (TXT, SEQS, HEADS * HD), 1.0, 6.0, ((2, 4),)),
        "text_values": scatter_about(splits[5], (TXT, SEQS, HEADS * HD), 1.0, 6.0, ((2, 4),)),
        "text_mask": place_ends((jax.random.randint(splits[6], (TXT, SEQS), 0, 4) < 3).astype(jnp.int32), jax.random.fold_in(splits[6], 1), 0, 1),
    }


masked_fill = -1.0e9


def settle(values):
    return lax.optimization_barrier(values.astype(jnp.bfloat16)).astype(jnp.float32)


def reference(inputs, out_grad, qkv_weight, out_weight, text_keys, text_values, text_mask):
    model_width = HEADS * HD
    score_scale = HD ** -0.5
    total_rows = VIDEO * SEQS
    flat_inputs = inputs.reshape(total_rows, D)
    flat_grads = out_grad.reshape(total_rows, D)
    projected = jnp.dot(flat_inputs, qkv_weight.reshape(D, 3 * model_width), preferred_element_type=jnp.float32)
    projected = projected.astype(jnp.bfloat16).reshape(VIDEO, SEQS, 3, HEADS, HD)
    grad_attn = jnp.dot(flat_grads, out_weight, preferred_element_type=jnp.float32)
    grad_attn = grad_attn.astype(jnp.bfloat16).reshape(VIDEO, SEQS, HEADS, HD)
    text_valid = text_mask == 1
    key_valid = jnp.concatenate([text_valid, jnp.ones((VIDEO, SEQS), dtype=bool)], axis=0)
    head_items = (
        jnp.transpose(projected[:, :, 0], (2, 0, 1, 3)),
        jnp.transpose(projected[:, :, 1], (2, 0, 1, 3)),
        jnp.transpose(projected[:, :, 2], (2, 0, 1, 3)),
        jnp.transpose(grad_attn, (2, 0, 1, 3)),
        jnp.transpose(text_keys.reshape(TXT, SEQS, HEADS, HD), (2, 0, 1, 3)),
        jnp.transpose(text_values.reshape(TXT, SEQS, HEADS, HD), (2, 0, 1, 3)),
    )

    def one_head(head_arrays):
        query_all, key_video, value_video, grad_all, key_text, value_text = head_arrays
        key_rows = jnp.concatenate([key_text, key_video], axis=0).astype(jnp.float32)
        value_rows = jnp.concatenate([value_text, value_video], axis=0).astype(jnp.float32)
        valid_mask = key_valid.T[:, None, :]

        def per_block(sums, block_index):
            text_sum, video_sum = sums
            first_row = (block_index * VID_DEV).astype(jnp.int32)
            query_block = lax.dynamic_slice_in_dim(query_all, first_row, VID_DEV, 0).astype(jnp.float32)
            grad_block = lax.dynamic_slice_in_dim(grad_all, first_row, VID_DEV, 0).astype(jnp.float32)
            logits = jnp.einsum("vsd,lsd->svl", query_block, key_rows) * score_scale
            logits = jnp.where(valid_mask, logits, masked_fill)
            row_max = jnp.max(logits, axis=-1)
            raw_weights = jnp.exp(logits - row_max[..., None])
            total = jnp.sum(raw_weights, axis=-1)
            out_block = jnp.einsum("svl,lsd->vsd", settle(raw_weights), value_rows) / total.T[:, :, None]
            out_block = out_block.astype(jnp.bfloat16)
            log_total = row_max + jnp.log(total)
            row_dot = jnp.sum(grad_block * out_block.astype(jnp.float32), axis=-1)
            probabilities = jnp.exp(logits - log_total[..., None])
            grad_values = jnp.einsum("svl,vsd->lsd", settle(probabilities), grad_block)
            grad_probs = jnp.einsum("vsd,lsd->svl", grad_block, value_rows)
            grad_logits = settle(probabilities * (grad_probs - row_dot.T[..., None]) * score_scale)
            grad_query = jnp.einsum("svl,lsd->vsd", grad_logits, key_rows).astype(jnp.bfloat16)
            grad_keys = jnp.einsum("svl,vsd->lsd", grad_logits, query_block)
            key_term = jnp.stack([grad_keys, grad_values], axis=2)
            text_sum = text_sum + key_term[:TXT]
            video_sum = video_sum + settle(key_term[TXT:])
            return (text_sum, video_sum), (grad_query, out_block)

        start_sums = (jnp.zeros((TXT, SEQS, 2, HD), jnp.float32), jnp.zeros((VIDEO, SEQS, 2, HD), jnp.float32))
        final_sums, block_outputs = lax.scan(per_block, start_sums, jnp.arange(N_BLK, dtype=jnp.int32))
        grad_query = block_outputs[0].reshape(VIDEO, SEQS, HD)
        out_rows = block_outputs[1].reshape(VIDEO, SEQS, HD)
        return grad_query, out_rows, final_sums[0], final_sums[1].astype(jnp.bfloat16)

    grad_query, out_rows, text_sum, video_sum = lax.map(one_head, head_items)
    grad_query = jnp.transpose(grad_query, (1, 2, 0, 3)).reshape(VIDEO, SEQS, 1, model_width)
    attn_out = jnp.transpose(out_rows, (1, 2, 0, 3)).reshape(VIDEO, SEQS, model_width)
    video_kv = jnp.transpose(video_sum, (1, 2, 3, 0, 4)).reshape(VIDEO, SEQS, 2, model_width)
    text_kv = jnp.transpose(text_sum, (1, 2, 3, 0, 4)).reshape(TXT, SEQS, 2, model_width)
    grad_projected = jnp.concatenate([grad_query, video_kv], axis=2)
    flat_projected = grad_projected.reshape(total_rows, 3 * model_width)
    grad_inputs = jnp.dot(flat_projected, qkv_weight.reshape(D, 3 * model_width).T, preferred_element_type=jnp.float32)
    grad_inputs = grad_inputs.astype(jnp.bfloat16).reshape(VIDEO, SEQS, D)

    def weight_block(sums, block_index):
        qkv_sum, out_sum = sums
        first_row = (block_index * VID_DEV).astype(jnp.int32)
        input_block = lax.dynamic_slice_in_dim(inputs, first_row, VID_DEV, 0).reshape(VID_DEV * SEQS, D)
        grad_block = lax.dynamic_slice_in_dim(out_grad, first_row, VID_DEV, 0).reshape(VID_DEV * SEQS, D)
        projected_block = lax.dynamic_slice_in_dim(grad_projected, first_row, VID_DEV, 0).reshape(VID_DEV * SEQS, 3 * model_width)
        attn_block = lax.dynamic_slice_in_dim(attn_out, first_row, VID_DEV, 0).reshape(VID_DEV * SEQS, model_width)
        qkv_sum = qkv_sum + settle(jnp.dot(input_block.T, projected_block, preferred_element_type=jnp.float32))
        out_sum = out_sum + settle(jnp.dot(grad_block.T, attn_block, preferred_element_type=jnp.float32))
        return (qkv_sum, out_sum), None

    start_weights = (jnp.zeros((D, 3 * model_width), jnp.float32), jnp.zeros((D, model_width), jnp.float32))
    weight_sums, unused = lax.scan(weight_block, start_weights, jnp.arange(N_BLK, dtype=jnp.int32))
    grad_qkv_weight = weight_sums[0].reshape(D, 3, model_width)
    grad_out_weight = weight_sums[1]
    return grad_inputs, grad_qkv_weight, grad_out_weight, text_kv[:, :, 0], text_kv[:, :, 1]
```

```python
import jax
import jax.numpy as jnp
from jax import lax
from jax.experimental import pallas as pl
from jax.experimental.pallas import tpu as pltpu
from jax.sharding import PartitionSpec as P

HD = 128
MASKED = -1000000000.0
F32 = jnp.float32
BF16 = jnp.bfloat16
NY = 4
NZX = 8


def nt_dot(a, b):
    return lax.dot_general(a, b, (((1,), (1,)), ((), ())), preferred_element_type=F32)


def nn_dot(a, b):
    return lax.dot_general(a, b, (((1,), (0,)), ((), ())), preferred_element_type=F32)


def tn_dot(a, b):
    return lax.dot_general(a, b, (((0,), (0,)), ((), ())), preferred_element_type=F32)


def rows_of(ref):
    block = ref[...]
    return block.reshape(-1, block.shape[-1])


def pick(parts, value):
    return jnp.concatenate([rows_of(part) for part in parts] + [value], axis=0)


def scores(keys, q, valid, video):
    s = nt_dot(keys, q) * HD**-0.5
    return jnp.concatenate([s[:video], jnp.where(valid, s[video:], MASKED)], axis=0)


def stats_kernel(q_ref, g_ref, *refs):
    ks, vs = refs[:NY], refs[NY : 2 * NY]
    tk_ref, tv_ref, mask_ref, stat_ref, out_ref = refs[2 * NY :]
    q, g = rows_of(q_ref), rows_of(g_ref)
    k, v = pick(ks, tk_ref[...]), pick(vs, tv_ref[...])
    s = scores(k, q, mask_ref[:, 0:1] == 1, k.shape[0] - tk_ref.shape[0])
    top = jnp.max(s, axis=0, keepdims=True)
    p = jnp.exp(s - top)
    total = jnp.sum(p, axis=0, keepdims=True)
    stat_ref[0, 0:1, :] = top
    stat_ref[0, 1:2, :] = total
    stat_ref[0, 2:3, :] = jnp.sum(p * nt_dot(v, g), axis=0, keepdims=True)
    out = tn_dot(v, p.astype(BF16)) / total
    out_ref[...] = out.T.astype(BF16).reshape(out_ref.shape)


def merged(stat_ref):
    tops = [stat_ref[i, 0, 0:1, :] for i in range(NZX)]
    top = tops[0]
    for other in tops[1:]:
        top = jnp.maximum(top, other)
    total = jnp.zeros_like(top)
    dot = jnp.zeros_like(top)
    shares = []
    for i in range(NZX):
        factor = jnp.exp(tops[i] - top)
        shares.append(factor * stat_ref[i, 0, 1:2, :])
        total += shares[i]
        dot += factor * stat_ref[i, 0, 2:3, :]
    return top, total, dot / total, shares


def combine_kernel(out_ref, stat_ref, o_ref):
    _, total, _, shares = merged(stat_ref)
    rows = out_ref.shape[1]
    acc = jnp.zeros((rows, HD), F32)
    for i in range(NZX):
        weight = jnp.broadcast_to(shares[i] / total, (HD, rows)).T
        acc += weight * out_ref[i].astype(F32)
    o_ref[...] = acc.astype(BF16)


def grads_kernel(q_ref, g_ref, *refs):
    ks, vs = refs[:NY], refs[NY : 2 * NY]
    tk_ref, tv_ref, mask_ref, stat_ref, dq_ref = refs[2 * NY : 2 * NY + 5]
    kv_refs, acc_ref = refs[2 * NY + 5 : -1], refs[-1]
    step, steps = pl.program_id(1), pl.num_programs(1)
    q, g = rows_of(q_ref), rows_of(g_ref)
    k, v = pick(ks, tk_ref[...]), pick(vs, tv_ref[...])
    keys = k.shape[0] - tk_ref.shape[0]
    top, total, dot, _ = merged(stat_ref)
    s = scores(k, q, mask_ref[:, 0:1] == 1, keys)
    p = jnp.exp(s - (top + jnp.log(total)))
    ds = (p * (nt_dot(v, g) - dot) * HD**-0.5).astype(BF16)
    dq = tn_dot(k, ds)
    dq_ref[...] = dq.T.astype(BF16).reshape(dq_ref.shape)

    @pl.when(step == 0)
    def _():
        acc_ref[...] = jnp.zeros_like(acc_ref)

    acc_ref[0] += nn_dot(ds, q)
    acc_ref[1] += nn_dot(p.astype(BF16), g)

    @pl.when(step == steps - 1)
    def _():
        per = keys // NY
        text = (acc_ref.shape[1] - keys) // NY
        for y in range(NY):
            kv_ref = kv_refs[y]
            kv_ref[:per] = acc_ref[0, y * per : (y + 1) * per].astype(BF16)
            kv_ref[per : 2 * per] = acc_ref[1, y * per : (y + 1) * per].astype(BF16)
            at = keys + y * text
            kv_ref[2 * per :] = jnp.concatenate(
                [acc_ref[0, at : at + text], acc_ref[1, at : at + text]], axis=0
            ).astype(BF16)


def weights_kernel(*refs):
    xs, gs, o_ref = refs[:NY], refs[NY : 2 * NY], refs[2 * NY]
    acc = tn_dot(xs[0][...], rows_of(gs[0]))
    for y in range(1, NY):
        acc += tn_dot(xs[y][...], rows_of(gs[y]))
    o_ref[:, 0] = acc.astype(BF16).reshape(o_ref.shape[0], o_ref.shape[2], o_ref.shape[3])


def per_device(inputs, out_grad, qkv_weight, out_weight, text_keys, text_values, text_mask):
    rows = inputs.shape[0]
    part = inputs.shape[2]
    width = qkv_weight.shape[2]
    heads = width // HD
    text = text_keys.shape[0]
    blk = lax.axis_index("blk")
    head = lax.axis_index("head")
    zx, y_at = lax.rem(blk, NZX), blk // NZX
    core, z_hi = lax.rem(head, 2), head // 2
    along_zx = [[y * NZX + i for i in range(NZX)] for y in range(NY)]
    core_swap = [(i, i ^ 1) for i in range(4)]
    z_swap = [(i, i ^ 2) for i in range(4)]

    def exchange(array):
        return lax.all_to_all(array, "blk", 0, 0, tiled=True, axis_index_groups=along_zx)

    def spread(array):
        return exchange(jnp.broadcast_to(array[None], (NZX,) + array.shape))

    def shift(array, by):
        return lax.ppermute(
            array, "blk", [(i, (i + by * NZX) % (NY * NZX)) for i in range(NY * NZX)]
        )

    def around(array):
        return [array] + [shift(array, by) for by in range(1, NY)]

    def head_gather(own):
        far = lax.ppermute(own, "head", z_swap)
        near = lax.ppermute(own, "head", core_swap)
        far_near = lax.ppermute(far, "head", core_swap)
        return [
            jnp.where(
                z_hi == z,
                jnp.where(core == c, own, near),
                jnp.where(core == c, far, far_near),
            )
            for z in range(2)
            for c in range(2)
        ]

    def slices_around(parts):
        def slice_for(y):
            return jnp.where(
                y < 2, jnp.where(y == 0, parts[0], parts[1]), jnp.where(y == 2, parts[2], parts[3])
            )

        own = slice_for(y_at)
        return [own] + [shift(slice_for(lax.rem(y_at + by, NY)), by) for by in range(1, NY)]

    in_parts = head_gather(inputs[:, 0])
    grad_parts = head_gather(out_grad[:, 0])
    projected = jnp.einsum(
        "vd,dch->cvh", jnp.concatenate(in_parts, axis=1), qkv_weight, preferred_element_type=F32
    ).astype(BF16)
    grad_attn = jnp.dot(
        jnp.concatenate(grad_parts, axis=1), out_weight, preferred_element_type=F32
    ).astype(BF16)

    kv_all = around(projected[1:])
    qg_all = spread(jnp.stack([projected[0], grad_attn]))

    text_own = text // (NY * NZX)
    text_per = NY * text_own
    slot = lax.broadcasted_iota(jnp.int32, (text_per, text), 0)
    source = lax.broadcasted_iota(jnp.int32, (text_per, text), 1)
    wanted = (lax.rem(y_at + NY - slot // text_own, NY) * NZX + zx) * text_own + lax.rem(
        slot, text_own
    )
    chosen = source == wanted
    select = chosen.astype(BF16)
    tk = jnp.dot(select, text_keys[:, 0], preferred_element_type=F32).astype(BF16)
    tv = jnp.dot(select, text_values[:, 0], preferred_element_type=F32).astype(BF16)
    mask = jnp.sum(jnp.where(chosen, text_mask[:, 0][None, :], 0), axis=1, keepdims=True)
    mask = jnp.broadcast_to(mask, (text_per, HD))

    half = NZX // 2
    q_rows = half * rows
    steps = NZX // half
    grid = (heads, steps)
    params = pltpu.CompilerParams(
        vmem_limit_bytes=56 * 1024 * 1024, dimension_semantics=("arbitrary", "arbitrary")
    )
    in_specs = (
        [
            pl.BlockSpec((half, 1, rows, HD), lambda h, i: (i, 0, 0, h)),
            pl.BlockSpec((half, 1, rows, HD), lambda h, i: (i, 1, 0, h)),
        ]
        + [pl.BlockSpec((1, rows, HD), lambda h, i: (0, 0, h))] * NY
        + [pl.BlockSpec((1, rows, HD), lambda h, i: (1, 0, h))] * NY
        + [
            pl.BlockSpec((text_per, HD), lambda h, i: (0, h)),
            pl.BlockSpec((text_per, HD), lambda h, i: (0, h)),
            pl.BlockSpec((text_per, HD), lambda h, i: (0, 0)),
        ]
    )
    x_in = slices_around(in_parts)
    x_grad = slices_around(grad_parts)
    operands = (qg_all, qg_all, *kv_all, *kv_all, tk, tv, mask)
    stats, out_terms = pl.pallas_call(
        stats_kernel,
        grid=grid,
        in_specs=in_specs,
        out_specs=[
            pl.BlockSpec((1, 3, q_rows), lambda h, i: (h, 0, i)),
            pl.BlockSpec((half, rows, HD), lambda h, i: (i, 0, h)),
        ],
        out_shape=[
            jax.ShapeDtypeStruct((heads, 3, steps * q_rows), F32),
            jax.ShapeDtypeStruct((NZX, rows, width), BF16),
        ],
        compiler_params=params,
        name="attention_stats",
    )(*operands)
    all_stats = spread(stats)
    out_all = exchange(out_terms)
    own_stats = lax.dynamic_index_in_dim(
        all_stats.reshape(NZX, heads, 3, NZX, rows), zx, 3, keepdims=False
    )
    attn_out = pl.pallas_call(
        combine_kernel,
        grid=(heads,),
        in_specs=[
            pl.BlockSpec((NZX, rows, HD), lambda h: (0, 0, h)),
            pl.BlockSpec((NZX, 1, 3, rows), lambda h: (0, h, 0, 0)),
        ],
        out_specs=pl.BlockSpec((rows, HD), lambda h: (0, h)),
        out_shape=jax.ShapeDtypeStruct((rows, width), BF16),
        compiler_params=pltpu.CompilerParams(vmem_limit_bytes=56 * 1024 * 1024),
        name="combine_out",
    )(out_all, own_stats)

    kv_rows = 2 * rows + 2 * text_own
    dq_terms, *kv_terms = pl.pallas_call(
        grads_kernel,
        grid=grid,
        in_specs=in_specs + [pl.BlockSpec((NZX, 1, 3, q_rows), lambda h, i: (0, h, 0, i))],
        out_specs=[pl.BlockSpec((half, rows, HD), lambda h, i: (i, 0, h))]
        + [pl.BlockSpec((kv_rows, HD), lambda h, i: (0, h))] * NY,
        out_shape=[jax.ShapeDtypeStruct((NZX, rows, width), BF16)]
        + [jax.ShapeDtypeStruct((kv_rows, width), BF16)] * NY,
        scratch_shapes=[pltpu.VMEM((2, NY * rows + text_per, HD), F32)],
        compiler_params=params,
        name="attention_grads",
    )(*operands, all_stats)

    kv_sum = kv_terms[0].astype(F32)
    for by in range(1, NY):
        kv_sum += shift(kv_terms[by], NY - by).astype(F32)
    dq = jnp.sum(exchange(dq_terms).astype(F32), axis=0).astype(BF16)
    kv = kv_sum[: 2 * rows].astype(BF16).reshape(2, rows, width)
    text_sum = kv_sum[2 * rows :].reshape(2, text_own, 1, width)
    grad_projected = jnp.concatenate([dq[None], kv])

    own = part // NZX

    def weight_grad(xs, gs):
        count = gs[0].shape[0]
        terms = pl.pallas_call(
            weights_kernel,
            grid=(count,),
            in_specs=[pl.BlockSpec((rows, part), lambda c: (0, 0))] * NY
            + [pl.BlockSpec((1, rows, width), lambda c: (c, 0, 0))] * NY,
            out_specs=pl.BlockSpec((NZX, 1, own, width), lambda c: (0, c, 0, 0)),
            out_shape=jax.ShapeDtypeStruct((NZX, count, own, width), BF16),
            compiler_params=pltpu.CompilerParams(vmem_limit_bytes=56 * 1024 * 1024),
            name="weight_grads",
        )(*xs, *gs)
        return jnp.sum(exchange(terms).astype(F32), axis=0)

    out_sum = weight_grad(x_grad, around(attn_out[None]))
    qkv_sum = weight_grad(x_in, around(grad_projected))

    terms = jnp.einsum(
        "cvh,sdch->svd",
        grad_projected,
        qkv_weight.reshape(4, part, 3, width),
        preferred_element_type=F32,
    ).astype(BF16)
    keep = [jnp.where(core == 0, terms[2 * z], terms[2 * z + 1]) for z in range(2)]
    give = [jnp.where(core == 0, terms[2 * z + 1], terms[2 * z]) for z in range(2)]
    pair = [
        keep[z].astype(F32) + lax.ppermute(give[z], "head", core_swap).astype(F32)
        for z in range(2)
    ]
    mine = jnp.where(z_hi == 0, pair[0], pair[1])
    other = jnp.where(z_hi == 0, pair[1], pair[0]).astype(BF16)
    grad_inputs = (mine + lax.ppermute(other, "head", z_swap).astype(F32)).astype(BF16)

    return (
        grad_inputs[:, None],
        jnp.transpose(qkv_sum, (1, 0, 2)),
        out_sum[0],
        text_sum[0],
        text_sum[1],
    )


def solution(mesh):
    return jax.shard_map(
        per_device,
        mesh=mesh,
        in_specs=(
            P("blk", None, "head"),
            P("blk", None, "head"),
            P(None, None, "head"),
            P(None, "head"),
            P(None, None, "head"),
            P(None, None, "head"),
            P(),
        ),
        out_specs=(
            P("blk", None, "head"),
            P("blk", None, "head"),
            P("blk", "head"),
            P("blk", None, "head"),
            P("blk", None, "head"),
        ),
        check_vma=False,
    )
```

```python
import jax
import jax.numpy as jnp
from jax import lax
from jax.experimental import pallas as pl
from jax.experimental.pallas import tpu as pltpu
from jax.sharding import PartitionSpec as P

HD = 128
LOG2E = 1.4426950408889634
MASKED = -1000000000.0 * LOG2E
F32 = jnp.float32
BF16 = jnp.bfloat16
NY = 4
NZX = 8


def nt_dot(a, b):
    return lax.dot_general(a, b, (((1,), (1,)), ((), ())), preferred_element_type=F32)


def nn_dot(a, b):
    return lax.dot_general(a, b, (((1,), (0,)), ((), ())), preferred_element_type=F32)


def tn_dot(a, b):
    return lax.dot_general(a, b, (((0,), (0,)), ((), ())), preferred_element_type=F32)


def rows_of(ref):
    block = ref[...]
    return block.reshape(-1, block.shape[-1])


def pick(parts, value):
    return jnp.concatenate([rows_of(part) for part in parts] + [value], axis=0)


def scores(keys, q, valid, video):
    s = nt_dot(keys, q) * (HD**-0.5 * LOG2E)
    return jnp.concatenate([s[:video], jnp.where(valid, s[video:], MASKED)], axis=0)


def stats_kernel(q_ref, g_ref, *refs):
    ks, vs = refs[:NY], refs[NY : 2 * NY]
    tk_ref, tv_ref, mask_ref, stat_ref, out_ref = refs[2 * NY :]
    q, g = rows_of(q_ref), rows_of(g_ref)
    k, v = pick(ks, tk_ref[...]), pick(vs, tv_ref[...])
    s = scores(k, q, mask_ref[:, 0:1] == 1, k.shape[0] - tk_ref.shape[0])
    top = jnp.max(s, axis=0, keepdims=True)
    p = jnp.exp2(s - top)
    total = jnp.sum(p, axis=0, keepdims=True)
    stat_ref[0, 0:1, :] = top + jnp.log2(total)
    stat_ref[0, 1:2, :] = jnp.sum(p * nt_dot(v, g), axis=0, keepdims=True) / total
    out = tn_dot(v, p.astype(BF16)) / total
    out_ref[...] = out.T.astype(BF16).reshape(out_ref.shape)


def merged(stat_ref):
    logs = [stat_ref[i, 0, 0:1, :] for i in range(NZX)]
    top = logs[0]
    for other in logs[1:]:
        top = jnp.maximum(top, other)
    shares = [jnp.exp2(log - top) for log in logs]
    total = sum(shares[1:], shares[0])
    dot = shares[0] * stat_ref[0, 0, 1:2, :]
    for i in range(1, NZX):
        dot += shares[i] * stat_ref[i, 0, 1:2, :]
    return top + jnp.log2(total), dot / total, shares, total


def combine_kernel(out_ref, stat_ref, o_ref):
    _, _, shares, total = merged(stat_ref)
    rows = out_ref.shape[1]
    acc = jnp.zeros((rows, HD), F32)
    for i in range(NZX):
        weight = jnp.broadcast_to(shares[i] / total, (HD, rows)).T
        acc += weight * out_ref[i].astype(F32)
    o_ref[...] = acc.astype(BF16)


def grads_kernel(q_ref, g_ref, *refs):
    ks, vs = refs[:NY], refs[NY : 2 * NY]
    tk_ref, tv_ref, mask_ref, stat_ref, dq_ref = refs[2 * NY : 2 * NY + 5]
    kv_refs, acc_ref = refs[2 * NY + 5 : -1], refs[-1]
    step, steps = pl.program_id(1), pl.num_programs(1)
    q, g = rows_of(q_ref), rows_of(g_ref)
    k, v = pick(ks, tk_ref[...]), pick(vs, tv_ref[...])
    keys = k.shape[0] - tk_ref.shape[0]
    log_total, dot, _, _ = merged(stat_ref)
    s = scores(k, q, mask_ref[:, 0:1] == 1, keys)
    p = jnp.exp2(s - log_total)
    ds = (p * (nt_dot(v, g) - dot)).astype(BF16)
    dq = tn_dot(k, ds) * HD**-0.5
    dq_ref[...] = dq.T.astype(BF16).reshape(dq_ref.shape)

    @pl.when(step == 0)
    def _():
        acc_ref[...] = jnp.zeros_like(acc_ref)

    acc_ref[0] += nn_dot(ds, q)
    acc_ref[1] += nn_dot(p.astype(BF16), g)

    @pl.when(step == steps - 1)
    def _():
        per = keys // NY
        text = (acc_ref.shape[1] - keys) // NY
        for y in range(NY):
            kv_ref = kv_refs[y]
            kv_ref[:per] = (acc_ref[0, y * per : (y + 1) * per] * HD**-0.5).astype(BF16)
            kv_ref[per : 2 * per] = acc_ref[1, y * per : (y + 1) * per].astype(BF16)
            at = keys + y * text
            kv_ref[2 * per :] = jnp.concatenate(
                [acc_ref[0, at : at + text] * HD**-0.5, acc_ref[1, at : at + text]], axis=0
            ).astype(BF16)


def weights_kernel(*refs):
    xs, gs, o_ref = refs[:NY], refs[NY:-1], refs[-1]

    def store(gs):
        acc = tn_dot(xs[0][...], rows_of(gs[0]))
        for y in range(1, NY):
            acc += tn_dot(xs[y][...], rows_of(gs[y]))
        o_ref[:, 0] = acc.astype(BF16).reshape(o_ref.shape[0], o_ref.shape[2], o_ref.shape[3])

    if len(gs) == NY:
        store(gs)
    else:
        first = pl.program_id(0) == 0
        pl.when(first)(lambda: store(gs[:NY]))
        pl.when(jnp.logical_not(first))(lambda: store(gs[NY:]))


def per_device(inputs, out_grad, qkv_weight, out_weight, text_keys, text_values, text_mask):
    rows = inputs.shape[0]
    part = inputs.shape[2]
    width = qkv_weight.shape[2]
    heads = width // HD
    text = text_keys.shape[0]
    blk = lax.axis_index("blk")
    head = lax.axis_index("head")
    zx, y_at = lax.rem(blk, NZX), blk // NZX
    core, z_hi = lax.rem(head, 2), head // 2
    along_zx = [[y * NZX + i for i in range(NZX)] for y in range(NY)]
    core_swap = [(i, i ^ 1) for i in range(4)]
    z_swap = [(i, i ^ 2) for i in range(4)]

    def exchange(array):
        return lax.all_to_all(array, "blk", 0, 0, tiled=True, axis_index_groups=along_zx)

    def spread(array):
        return exchange(jnp.broadcast_to(array[None], (NZX,) + array.shape))

    def shift(array, by):
        return lax.ppermute(
            array, "blk", [(i, (i + by * NZX) % (NY * NZX)) for i in range(NY * NZX)]
        )

    def around(array):
        return [array] + [shift(array, by) for by in range(1, NY)]

    def head_gather(own, far):
        near = lax.ppermute(own, "head", core_swap)
        far_near = lax.ppermute(far, "head", core_swap)
        return [
            jnp.where(
                z_hi == z,
                jnp.where(core == c, own, near),
                jnp.where(core == c, far, far_near),
            )
            for z in range(2)
            for c in range(2)
        ]

    def slices_around(parts):
        def slice_for(y):
            return jnp.where(
                y < 2, jnp.where(y == 0, parts[0], parts[1]), jnp.where(y == 2, parts[2], parts[3])
            )

        own = slice_for(y_at)
        return [own] + [shift(slice_for(lax.rem(y_at + by, NY)), by) for by in range(1, NY)]

    far_in = lax.ppermute(inputs[:, 0], "head", z_swap)
    far_grad = lax.ppermute(out_grad[:, 0], "head", z_swap)
    in_parts = head_gather(inputs[:, 0], far_in)
    projected = jnp.einsum(
        "vd,dch->cvh", jnp.concatenate(in_parts, axis=1), qkv_weight, preferred_element_type=F32
    ).astype(BF16)
    far_grad, projected = lax.optimization_barrier((far_grad, projected))
    grad_parts = head_gather(out_grad[:, 0], far_grad)
    grad_attn = jnp.dot(
        jnp.concatenate(grad_parts, axis=1), out_weight, preferred_element_type=F32
    ).astype(BF16)

    kv_all = around(projected[1:])
    qg_all = spread(jnp.stack([projected[0], grad_attn]))

    text_own = text // (NY * NZX)
    text_per = NY * text_own
    slot = lax.broadcasted_iota(jnp.int32, (text_per, text), 0)
    source = lax.broadcasted_iota(jnp.int32, (text_per, text), 1)
    wanted = (lax.rem(y_at + NY - slot // text_own, NY) * NZX + zx) * text_own + lax.rem(
        slot, text_own
    )
    chosen = source == wanted
    select = chosen.astype(BF16)
    tk = jnp.dot(select, text_keys[:, 0], preferred_element_type=F32).astype(BF16)
    tv = jnp.dot(select, text_values[:, 0], preferred_element_type=F32).astype(BF16)
    mask = jnp.sum(jnp.where(chosen, text_mask[:, 0][None, :], 0), axis=1, keepdims=True)
    mask = jnp.broadcast_to(mask, (text_per, HD))

    half = NZX // 2
    q_rows = half * rows
    steps = NZX // half
    grid = (heads, steps)
    params = pltpu.CompilerParams(
        vmem_limit_bytes=56 * 1024 * 1024, dimension_semantics=("arbitrary", "arbitrary")
    )
    in_specs = (
        [
            pl.BlockSpec((half, 1, rows, HD), lambda h, i: (i, 0, 0, h)),
            pl.BlockSpec((half, 1, rows, HD), lambda h, i: (i, 1, 0, h)),
        ]
        + [pl.BlockSpec((1, rows, HD), lambda h, i: (0, 0, h))] * NY
        + [pl.BlockSpec((1, rows, HD), lambda h, i: (1, 0, h))] * NY
        + [
            pl.BlockSpec((text_per, HD), lambda h, i: (0, h)),
            pl.BlockSpec((text_per, HD), lambda h, i: (0, h)),
            pl.BlockSpec((text_per, HD), lambda h, i: (0, 0)),
        ]
    )
    x_in = slices_around(in_parts)
    x_grad = slices_around(grad_parts)
    operands = (qg_all, qg_all, *kv_all, *kv_all, tk, tv, mask)
    stats, out_terms = pl.pallas_call(
        stats_kernel,
        grid=grid,
        in_specs=in_specs,
        out_specs=[
            pl.BlockSpec((1, 2, q_rows), lambda h, i: (h, 0, i)),
            pl.BlockSpec((half, rows, HD), lambda h, i: (i, 0, h)),
        ],
        out_shape=[
            jax.ShapeDtypeStruct((heads, 2, steps * q_rows), F32),
            jax.ShapeDtypeStruct((NZX, rows, width), BF16),
        ],
        compiler_params=params,
        name="attention_stats",
    )(*operands)
    stats, x_in, x_grad = lax.optimization_barrier((stats, x_in, x_grad))
    all_stats = spread(stats)
    out_all = exchange(out_terms)
    own_stats = lax.dynamic_slice_in_dim(all_stats, zx * rows, rows, 3)
    attn_out = pl.pallas_call(
        combine_kernel,
        grid=(heads,),
        in_specs=[
            pl.BlockSpec((NZX, rows, HD), lambda h: (0, 0, h)),
            pl.BlockSpec((NZX, 1, 2, rows), lambda h: (0, h, 0, 0)),
        ],
        out_specs=pl.BlockSpec((rows, HD), lambda h: (0, h)),
        out_shape=jax.ShapeDtypeStruct((rows, width), BF16),
        compiler_params=pltpu.CompilerParams(vmem_limit_bytes=56 * 1024 * 1024),
        name="combine_out",
    )(out_all, own_stats)

    kv_rows = 2 * rows + 2 * text_own
    dq_terms, *kv_terms = pl.pallas_call(
        grads_kernel,
        grid=grid,
        in_specs=in_specs + [pl.BlockSpec((NZX, 1, 2, q_rows), lambda h, i: (0, h, 0, i))],
        out_specs=[pl.BlockSpec((half, rows, HD), lambda h, i: (i, 0, h))]
        + [pl.BlockSpec((kv_rows, HD), lambda h, i: (0, h))] * NY,
        out_shape=[jax.ShapeDtypeStruct((NZX, rows, width), BF16)]
        + [jax.ShapeDtypeStruct((kv_rows, width), BF16)] * NY,
        scratch_shapes=[pltpu.VMEM((2, NY * rows + text_per, HD), F32)],
        compiler_params=params,
        name="attention_grads",
    )(*operands, all_stats)

    kv_sum = kv_terms[0].astype(F32)
    for by in range(1, NY):
        kv_sum += shift(kv_terms[by], NY - by).astype(F32)
    dq = jnp.sum(exchange(dq_terms).astype(F32), axis=0).astype(BF16)
    kv = kv_sum[: 2 * rows].astype(BF16).reshape(2, rows, width)
    text_sum = kv_sum[2 * rows :].reshape(2, text_own, 1, width)
    grad_projected = jnp.concatenate([dq[None], kv])

    own = part // NZX

    def weight_grad(xs, gs, more=()):
        count = 1 + (more[0].shape[0] if more else 0)
        terms = pl.pallas_call(
            weights_kernel,
            grid=(count,),
            in_specs=[pl.BlockSpec((rows, part), lambda c: (0, 0))] * NY
            + [pl.BlockSpec((1, rows, width), lambda c: (0, 0, 0))] * NY
            + [pl.BlockSpec((1, rows, width), lambda c: (jnp.maximum(c - 1, 0), 0, 0))] * len(more),
            out_specs=pl.BlockSpec((NZX, 1, own, width), lambda c: (0, c, 0, 0)),
            out_shape=jax.ShapeDtypeStruct((NZX, count, own, width), BF16),
            compiler_params=pltpu.CompilerParams(vmem_limit_bytes=56 * 1024 * 1024),
            name="weight_grads",
        )(*xs, *gs, *more)
        return jnp.sum(exchange(terms).astype(F32), axis=0)

    outs, kv = lax.optimization_barrier((around(attn_out[None]), kv))
    out_sum = weight_grad(x_grad, outs)
    qkv_sum = weight_grad(x_in, around(dq[None]), around(kv))

    terms = jnp.einsum(
        "cvh,sdch->svd",
        grad_projected,
        qkv_weight.reshape(4, part, 3, width),
        preferred_element_type=F32,
    ).astype(BF16)
    keep = [jnp.where(core == 0, terms[2 * z], terms[2 * z + 1]) for z in range(2)]
    give = [jnp.where(core == 0, terms[2 * z + 1], terms[2 * z]) for z in range(2)]
    pair = [
        keep[z].astype(F32) + lax.ppermute(give[z], "head", core_swap).astype(F32)
        for z in range(2)
    ]
    mine = jnp.where(z_hi == 0, pair[0], pair[1])
    other = jnp.where(z_hi == 0, pair[1], pair[0]).astype(BF16)
    grad_inputs = (mine + lax.ppermute(other, "head", z_swap).astype(F32)).astype(BF16)

    return (
        grad_inputs[:, None],
        jnp.transpose(qkv_sum, (1, 0, 2)),
        out_sum[0],
        text_sum[0],
        text_sum[1],
    )


def solution(mesh):
    return jax.shard_map(
        per_device,
        mesh=mesh,
        in_specs=(
            P("blk", None, "head"),
            P("blk", None, "head"),
            P(None, None, "head"),
            P(None, "head"),
            P(None, None, "head"),
            P(None, None, "head"),
            P(),
        ),
        out_specs=(
            P("blk", None, "head"),
            P("blk", None, "head"),
            P("blk", "head"),
            P("blk", None, "head"),
            P("blk", None, "head"),
        ),
        check_vma=False,
    )
```

```python
import jax
import jax.numpy as jnp
from jax import lax
from jax.experimental import pallas as pl
from jax.experimental.pallas import tpu as pltpu
from jax.sharding import PartitionSpec as P

HD = 128
LOG2E = 1.4426950408889634
MASKED = -1000000000.0 * LOG2E
F32 = jnp.float32
BF16 = jnp.bfloat16
NY = 4
NZX = 8


def nt_dot(a, b):
    return lax.dot_general(a, b, (((1,), (1,)), ((), ())), preferred_element_type=F32)


def nn_dot(a, b):
    return lax.dot_general(a, b, (((1,), (0,)), ((), ())), preferred_element_type=F32)


def tn_dot(a, b):
    return lax.dot_general(a, b, (((0,), (0,)), ((), ())), preferred_element_type=F32)


def rows_of(ref):
    block = ref[...]
    return block.reshape(-1, block.shape[-1])


def pick(parts, value):
    return jnp.concatenate([rows_of(part) for part in parts] + [value], axis=0)


def scores(keys, q, valid, video):
    s = nt_dot(keys, q) * (HD**-0.5 * LOG2E)
    return jnp.concatenate([s[:video], jnp.where(valid, s[video:], MASKED)], axis=0)


def stats_kernel(q_ref, g_ref, *refs):
    ks, vs = refs[:NY], refs[NY : 2 * NY]
    tk_ref, tv_ref, mask_ref, stat_ref, out_ref = refs[2 * NY :]
    q, g = rows_of(q_ref), rows_of(g_ref)
    k, v = pick(ks, tk_ref[...]), pick(vs, tv_ref[...])
    s = scores(k, q, mask_ref[:, 0:1] == 1, k.shape[0] - tk_ref.shape[0])
    top = jnp.max(s, axis=0, keepdims=True)
    p = jnp.exp2(s - top)
    total = jnp.sum(p, axis=0, keepdims=True)
    stat_ref[0, 0:1, :] = top + jnp.log2(total)
    stat_ref[0, 1:2, :] = jnp.sum(p * nt_dot(v, g), axis=0, keepdims=True) / total
    out = tn_dot(v, p.astype(BF16)) / total
    out_ref[...] = out.T.astype(BF16).reshape(out_ref.shape)


def merged(stat_ref):
    logs = [stat_ref[i, 0, 0:1, :] for i in range(NZX)]
    top = logs[0]
    for other in logs[1:]:
        top = jnp.maximum(top, other)
    shares = [jnp.exp2(log - top) for log in logs]
    total = sum(shares[1:], shares[0])
    dot = shares[0] * stat_ref[0, 0, 1:2, :]
    for i in range(1, NZX):
        dot += shares[i] * stat_ref[i, 0, 1:2, :]
    return top + jnp.log2(total), dot / total, shares, total


def combine_kernel(out_ref, stat_ref, o_ref):
    _, _, shares, total = merged(stat_ref)
    rows = out_ref.shape[1]
    acc = jnp.zeros((rows, HD), F32)
    for i in range(NZX):
        weight = jnp.broadcast_to(shares[i] / total, (HD, rows)).T
        acc += weight * out_ref[i].astype(F32)
    o_ref[...] = acc.astype(BF16)


def grads_kernel(q_ref, g_ref, *refs):
    ks, vs = refs[:NY], refs[NY : 2 * NY]
    tk_ref, tv_ref, mask_ref, stat_ref, dq_ref = refs[2 * NY : 2 * NY + 5]
    kv_refs, acc_ref = refs[2 * NY + 5 : -1], refs[-1]
    step, steps = pl.program_id(1), pl.num_programs(1)
    q, g = rows_of(q_ref), rows_of(g_ref)
    k, v = pick(ks, tk_ref[...]), pick(vs, tv_ref[...])
    keys = k.shape[0] - tk_ref.shape[0]
    log_total, dot, _, _ = merged(stat_ref)
    s = scores(k, q, mask_ref[:, 0:1] == 1, keys)
    p = jnp.exp2(s - log_total)
    ds = (p * (nt_dot(v, g) - dot)).astype(BF16)
    dq = tn_dot(k, ds) * HD**-0.5
    dq_ref[...] = dq.T.astype(BF16).reshape(dq_ref.shape)

    @pl.when(step == 0)
    def _():
        acc_ref[...] = jnp.zeros_like(acc_ref)

    acc_ref[0] += nn_dot(ds, q)
    acc_ref[1] += nn_dot(p.astype(BF16), g)

    @pl.when(step == steps - 1)
    def _():
        per = keys // NY
        text = (acc_ref.shape[1] - keys) // NY
        for y in range(NY):
            kv_ref = kv_refs[y]
            kv_ref[:per] = (acc_ref[0, y * per : (y + 1) * per] * HD**-0.5).astype(BF16)
            kv_ref[per : 2 * per] = acc_ref[1, y * per : (y + 1) * per].astype(BF16)
            at = keys + y * text
            kv_ref[2 * per :] = jnp.concatenate(
                [acc_ref[0, at : at + text] * HD**-0.5, acc_ref[1, at : at + text]], axis=0
            ).astype(BF16)


def weights_kernel(*refs):
    xs, gs, o_ref = refs[:NY], refs[NY:-1], refs[-1]
    acc = None
    for y in range(NY):
        g = [gs[y][c] for c in range(gs[y].shape[0])]
        term = tn_dot(xs[y][...], g[0] if len(g) == 1 else jnp.concatenate(g, axis=1))
        acc = term if acc is None else acc + term
    width = o_ref.shape[3]
    for c in range(o_ref.shape[1]):
        part = acc[:, c * width : (c + 1) * width].astype(BF16)
        o_ref[:, c] = part.reshape(o_ref.shape[0], o_ref.shape[2], width)


def per_device(inputs, out_grad, qkv_weight, out_weight, text_keys, text_values, text_mask):
    rows = inputs.shape[0]
    part = inputs.shape[2]
    width = qkv_weight.shape[2]
    heads = width // HD
    text = text_keys.shape[0]
    blk = lax.axis_index("blk")
    head = lax.axis_index("head")
    zx, y_at = lax.rem(blk, NZX), blk // NZX
    core, z_hi = lax.rem(head, 2), head // 2
    along_zx = [[y * NZX + i for i in range(NZX)] for y in range(NY)]
    core_swap = [(i, i ^ 1) for i in range(4)]
    z_swap = [(i, i ^ 2) for i in range(4)]

    def exchange(array):
        return lax.all_to_all(array, "blk", 0, 0, tiled=True, axis_index_groups=along_zx)

    def spread(array):
        return exchange(jnp.broadcast_to(array[None], (NZX,) + array.shape))

    def shift(array, by):
        return lax.ppermute(
            array, "blk", [(i, (i + by * NZX) % (NY * NZX)) for i in range(NY * NZX)]
        )

    def around(array):
        return [array] + [shift(array, by) for by in range(1, NY)]

    def head_gather(own, far):
        near = lax.ppermute(own, "head", core_swap)
        far_near = lax.ppermute(far, "head", core_swap)
        return [
            jnp.where(
                z_hi == z,
                jnp.where(core == c, own, near),
                jnp.where(core == c, far, far_near),
            )
            for z in range(2)
            for c in range(2)
        ]

    def slices_around(parts):
        def slice_for(y):
            return jnp.where(
                y < 2, jnp.where(y == 0, parts[0], parts[1]), jnp.where(y == 2, parts[2], parts[3])
            )

        own = slice_for(y_at)
        return [own] + [shift(slice_for(lax.rem(y_at + by, NY)), by) for by in range(1, NY)]

    far_in = lax.ppermute(inputs[:, 0], "head", z_swap)
    far_grad = lax.ppermute(out_grad[:, 0], "head", z_swap)
    in_parts = head_gather(inputs[:, 0], far_in)
    projected = jnp.einsum(
        "vd,dch->cvh", jnp.concatenate(in_parts, axis=1), qkv_weight, preferred_element_type=F32
    ).astype(BF16)
    far_grad, projected = lax.optimization_barrier((far_grad, projected))
    grad_parts = head_gather(out_grad[:, 0], far_grad)
    grad_attn = jnp.dot(
        jnp.concatenate(grad_parts, axis=1), out_weight, preferred_element_type=F32
    ).astype(BF16)

    kv_all = around(projected[1:])
    qg_all = spread(jnp.stack([projected[0], grad_attn]))

    text_own = text // (NY * NZX)
    text_per = NY * text_own
    slot = lax.broadcasted_iota(jnp.int32, (text_per, text), 0)
    source = lax.broadcasted_iota(jnp.int32, (text_per, text), 1)
    wanted = (lax.rem(y_at + NY - slot // text_own, NY) * NZX + zx) * text_own + lax.rem(
        slot, text_own
    )
    chosen = source == wanted
    select = chosen.astype(BF16)
    tk = jnp.dot(select, text_keys[:, 0], preferred_element_type=F32).astype(BF16)
    tv = jnp.dot(select, text_values[:, 0], preferred_element_type=F32).astype(BF16)
    mask = jnp.sum(jnp.where(chosen, text_mask[:, 0][None, :], 0), axis=1, keepdims=True)
    mask = jnp.broadcast_to(mask, (text_per, HD))

    half = NZX // 2
    q_rows = half * rows
    steps = NZX // half
    grid = (heads, steps)
    params = pltpu.CompilerParams(
        vmem_limit_bytes=56 * 1024 * 1024, dimension_semantics=("arbitrary", "arbitrary")
    )
    in_specs = (
        [
            pl.BlockSpec((half, 1, rows, HD), lambda h, i: (i, 0, 0, h)),
            pl.BlockSpec((half, 1, rows, HD), lambda h, i: (i, 1, 0, h)),
        ]
        + [pl.BlockSpec((1, rows, HD), lambda h, i: (0, 0, h))] * NY
        + [pl.BlockSpec((1, rows, HD), lambda h, i: (1, 0, h))] * NY
        + [
            pl.BlockSpec((text_per, HD), lambda h, i: (0, h)),
            pl.BlockSpec((text_per, HD), lambda h, i: (0, h)),
            pl.BlockSpec((text_per, HD), lambda h, i: (0, 0)),
        ]
    )
    x_in = slices_around(in_parts)
    kv_all, grad_parts = lax.optimization_barrier((kv_all, grad_parts))
    x_grad = slices_around(grad_parts)
    operands = (qg_all, qg_all, *kv_all, *kv_all, tk, tv, mask)
    stats, out_terms = pl.pallas_call(
        stats_kernel,
        grid=grid,
        in_specs=in_specs,
        out_specs=[
            pl.BlockSpec((1, 2, q_rows), lambda h, i: (h, 0, i)),
            pl.BlockSpec((half, rows, HD), lambda h, i: (i, 0, h)),
        ],
        out_shape=[
            jax.ShapeDtypeStruct((heads, 2, steps * q_rows), F32),
            jax.ShapeDtypeStruct((NZX, rows, width), BF16),
        ],
        compiler_params=params,
        name="attention_stats",
    )(*operands)
    stats, x_in, x_grad = lax.optimization_barrier((stats, x_in, x_grad))
    all_stats = spread(stats)
    out_all = exchange(out_terms)
    own_stats = lax.dynamic_slice_in_dim(all_stats, zx * rows, rows, 3)
    attn_out = pl.pallas_call(
        combine_kernel,
        grid=(heads,),
        in_specs=[
            pl.BlockSpec((NZX, rows, HD), lambda h: (0, 0, h)),
            pl.BlockSpec((NZX, 1, 2, rows), lambda h: (0, h, 0, 0)),
        ],
        out_specs=pl.BlockSpec((rows, HD), lambda h: (0, h)),
        out_shape=jax.ShapeDtypeStruct((rows, width), BF16),
        compiler_params=pltpu.CompilerParams(vmem_limit_bytes=56 * 1024 * 1024),
        name="combine_out",
    )(out_all, own_stats)

    kv_rows = 2 * rows + 2 * text_own
    dq_terms, *kv_terms = pl.pallas_call(
        grads_kernel,
        grid=grid,
        in_specs=in_specs + [pl.BlockSpec((NZX, 1, 2, q_rows), lambda h, i: (0, h, 0, i))],
        out_specs=[pl.BlockSpec((half, rows, HD), lambda h, i: (i, 0, h))]
        + [pl.BlockSpec((kv_rows, HD), lambda h, i: (0, h))] * NY,
        out_shape=[jax.ShapeDtypeStruct((NZX, rows, width), BF16)]
        + [jax.ShapeDtypeStruct((kv_rows, width), BF16)] * NY,
        scratch_shapes=[pltpu.VMEM((2, NY * rows + text_per, HD), F32)],
        compiler_params=params,
        name="attention_grads",
    )(*operands, all_stats)

    kv_sum = kv_terms[0].astype(F32)
    for by in range(1, NY):
        kv_sum += shift(kv_terms[by], NY - by).astype(F32)
    dq_all = exchange(dq_terms)
    kv = kv_sum[: 2 * rows].astype(BF16).reshape(2, rows, width)
    text_sum = kv_sum[2 * rows :].reshape(2, text_own, 1, width)

    own = part // NZX

    def weight_terms(xs, gs):
        count = gs[0].shape[0]
        return pl.pallas_call(
            weights_kernel,
            grid=(2,),
            in_specs=[pl.BlockSpec((rows, part // 2), lambda i: (0, i))] * NY
            + [pl.BlockSpec((count, rows, width), lambda i: (0, 0, 0))] * NY,
            out_specs=pl.BlockSpec((NZX // 2, count, own, width), lambda i: (i, 0, 0, 0)),
            out_shape=jax.ShapeDtypeStruct((NZX, count, own, width), BF16),
            compiler_params=pltpu.CompilerParams(vmem_limit_bytes=56 * 1024 * 1024),
            name="weight_grads",
        )(*xs, *gs)
    def total(array):
        return jnp.sum(array.astype(F32), axis=0)

    outs, kv = lax.optimization_barrier((around(attn_out[None]), kv))
    out_weights = weight_terms(x_grad, outs)
    kvs = around(kv)
    out_weights, first = lax.optimization_barrier((out_weights, kvs[1]))
    kvs = [kvs[0], first] + kvs[2:]
    out_received = exchange(out_weights)
    dq_all, kv = lax.optimization_barrier((dq_all, kv))
    dq = jnp.sum(dq_all.astype(F32), axis=0).astype(BF16)
    grad_projected = jnp.concatenate([dq[None], kv])
    terms = jnp.einsum(
        "cvh,sdch->svd",
        grad_projected,
        qkv_weight.reshape(4, part, 3, width),
        preferred_element_type=F32,
    ).astype(BF16)
    kvs, out_weights, terms = lax.optimization_barrier((kvs, out_weights, terms))
    kv_weights = weight_terms(x_in, kvs)
    kv_weights, out_received = lax.optimization_barrier((kv_weights, out_received))
    kv_received = exchange(kv_weights)

    dqs, kv_weights = lax.optimization_barrier((around(dq[None]), kv_weights))
    q_weights = weight_terms(x_in, dqs)
    q_weights, kv_received = lax.optimization_barrier((q_weights, kv_received))
    qkv_sum = jnp.concatenate([total(exchange(q_weights)), total(kv_received)])
    keep = [jnp.where(core == 0, terms[2 * z], terms[2 * z + 1]) for z in range(2)]
    give = [jnp.where(core == 0, terms[2 * z + 1], terms[2 * z]) for z in range(2)]
    pair = [
        keep[z].astype(F32) + lax.ppermute(give[z], "head", core_swap).astype(F32)
        for z in range(2)
    ]
    mine = jnp.where(z_hi == 0, pair[0], pair[1])
    other = jnp.where(z_hi == 0, pair[1], pair[0]).astype(BF16)
    grad_inputs = (mine + lax.ppermute(other, "head", z_swap).astype(F32)).astype(BF16)

    return (
        grad_inputs[:, None],
        jnp.transpose(qkv_sum, (1, 0, 2)),
        total(out_received)[0],
        text_sum[0],
        text_sum[1],
    )


def solution(mesh):
    return jax.shard_map(
        per_device,
        mesh=mesh,
        in_specs=(
            P("blk", None, "head"),
            P("blk", None, "head"),
            P(None, None, "head"),
            P(None, "head"),
            P(None, None, "head"),
            P(None, None, "head"),
            P(),
        ),
        out_specs=(
            P("blk", None, "head"),
            P("blk", None, "head"),
            P("blk", "head"),
            P("blk", None, "head"),
            P("blk", None, "head"),
        ),
        check_vma=False,
    )
```

```python
import jax
import jax.numpy as jnp
from jax import lax
from jax.experimental import pallas as pl
from jax.experimental.pallas import tpu as pltpu
from jax.sharding import PartitionSpec as P

HD = 128
LOG2E = 1.4426950408889634
MASKED = -1000000000.0 * LOG2E
F32 = jnp.float32
BF16 = jnp.bfloat16
NY = 4
NZX = 8


def nt_dot(a, b):
    return lax.dot_general(a, b, (((1,), (1,)), ((), ())), preferred_element_type=F32)


def nn_dot(a, b):
    return lax.dot_general(a, b, (((1,), (0,)), ((), ())), preferred_element_type=F32)


def tn_dot(a, b):
    return lax.dot_general(a, b, (((0,), (0,)), ((), ())), preferred_element_type=F32)


def rows_of(ref):
    block = ref[...]
    return block.reshape(-1, block.shape[-1])


def pick(parts, value):
    return jnp.concatenate([rows_of(part) for part in parts] + [value], axis=0)


def scores(keys, q, valid, video):
    s = nt_dot(keys, q) * (HD**-0.5 * LOG2E)
    return jnp.concatenate([s[:video], jnp.where(valid, s[video:], MASKED)], axis=0)


def stats_kernel(q_ref, g_ref, *refs):
    ks, vs = refs[:NY], refs[NY : 2 * NY]
    tk_ref, tv_ref, mask_ref, stat_ref, out_ref = refs[2 * NY :]
    q, g = rows_of(q_ref), rows_of(g_ref)
    k, v = pick(ks, tk_ref[...]), pick(vs, tv_ref[...])
    s = scores(k, q, mask_ref[:, 0:1] == 1, k.shape[0] - tk_ref.shape[0])
    top = jnp.max(s, axis=0, keepdims=True)
    p = jnp.exp2(s - top)
    total = jnp.sum(p, axis=0, keepdims=True)
    stat_ref[0, 0:1, :] = top + jnp.log2(total)
    stat_ref[0, 1:2, :] = jnp.sum(p * nt_dot(v, g), axis=0, keepdims=True) / total
    out = tn_dot(v, p.astype(BF16)) / total
    out_ref[...] = out.T.astype(BF16).reshape(out_ref.shape)


def merged(stat_ref):
    logs = [stat_ref[i, 0, 0:1, :] for i in range(NZX)]
    top = logs[0]
    for other in logs[1:]:
        top = jnp.maximum(top, other)
    shares = [jnp.exp2(log - top) for log in logs]
    total = sum(shares[1:], shares[0])
    dot = shares[0] * stat_ref[0, 0, 1:2, :]
    for i in range(1, NZX):
        dot += shares[i] * stat_ref[i, 0, 1:2, :]
    return top + jnp.log2(total), dot / total, shares, total


def combine_kernel(out_ref, stat_ref, o_ref):
    _, _, shares, total = merged(stat_ref)
    rows = out_ref.shape[1]
    acc = jnp.zeros((rows, HD), F32)
    for i in range(NZX):
        weight = jnp.broadcast_to(shares[i] / total, (HD, rows)).T
        acc += weight * out_ref[i].astype(F32)
    o_ref[...] = acc.astype(BF16)


def grads_kernel(q_ref, g_ref, *refs):
    ks, vs = refs[:NY], refs[NY : 2 * NY]
    tk_ref, tv_ref, mask_ref, stat_ref, dq_ref = refs[2 * NY : 2 * NY + 5]
    kv_refs = refs[2 * NY + 5 :]
    q, g = rows_of(q_ref), rows_of(g_ref)
    k, v = pick(ks, tk_ref[...]), pick(vs, tv_ref[...])
    keys = k.shape[0] - tk_ref.shape[0]
    log_total, dot, _, _ = merged(stat_ref)
    s = scores(k, q, mask_ref[:, 0:1] == 1, keys)
    p = jnp.exp2(s - log_total)
    ds = (p * (nt_dot(v, g) - dot)).astype(BF16)
    dq = tn_dot(k, ds) * HD**-0.5
    dq_ref[...] = dq.T.astype(BF16).reshape(dq_ref.shape)

    dk = nn_dot(ds, q) * HD**-0.5
    dv = nn_dot(p.astype(BF16), g)
    per = keys // NY
    text = (dk.shape[0] - keys) // NY
    for y in range(NY):
        own, at = slice(y * per, (y + 1) * per), slice(keys + y * text, keys + (y + 1) * text)
        kv_refs[y][:per] = dk[own].astype(BF16)
        kv_refs[y][per : 2 * per] = dv[own].astype(BF16)
        kv_refs[y][2 * per :] = jnp.concatenate([dk[at], dv[at]], axis=0).astype(BF16)


def weights_kernel(*refs):
    xs, gs, o_ref = refs[:NY], refs[NY:-1], refs[-1]
    acc = None
    for y in range(NY):
        g = [gs[y][c] for c in range(gs[y].shape[0])]
        term = tn_dot(xs[y][...], g[0] if len(g) == 1 else jnp.concatenate(g, axis=1))
        acc = term if acc is None else acc + term
    width = o_ref.shape[3]
    for c in range(o_ref.shape[1]):
        part = acc[:, c * width : (c + 1) * width].astype(BF16)
        o_ref[:, c] = part.reshape(o_ref.shape[0], o_ref.shape[2], width)


def per_device(inputs, out_grad, qkv_weight, out_weight, text_keys, text_values, text_mask):
    rows = inputs.shape[0]
    part = inputs.shape[2]
    width = qkv_weight.shape[2]
    heads = width // HD
    text = text_keys.shape[0]
    blk = lax.axis_index("blk")
    head = lax.axis_index("head")
    zx, y_at = lax.rem(blk, NZX), blk // NZX
    core, z_hi = lax.rem(head, 2), head // 2
    along_zx = [[y * NZX + i for i in range(NZX)] for y in range(NY)]
    core_swap = [(i, i ^ 1) for i in range(4)]
    z_swap = [(i, i ^ 2) for i in range(4)]

    def exchange(array):
        return lax.all_to_all(array, "blk", 0, 0, tiled=True, axis_index_groups=along_zx)

    def spread(array):
        return exchange(jnp.broadcast_to(array[None], (NZX,) + array.shape))

    def shift(array, by):
        return lax.ppermute(
            array, "blk", [(i, (i + by * NZX) % (NY * NZX)) for i in range(NY * NZX)]
        )

    def around(array):
        return [array] + [shift(array, by) for by in range(1, NY)]

    def head_gather(own, far):
        near = lax.ppermute(own, "head", core_swap)
        far_near = lax.ppermute(far, "head", core_swap)
        return [
            jnp.where(
                z_hi == z,
                jnp.where(core == c, own, near),
                jnp.where(core == c, far, far_near),
            )
            for z in range(2)
            for c in range(2)
        ]

    def slices_around(parts):
        def slice_for(y):
            return jnp.where(
                y < 2, jnp.where(y == 0, parts[0], parts[1]), jnp.where(y == 2, parts[2], parts[3])
            )

        own = slice_for(y_at)
        return [own] + [shift(slice_for(lax.rem(y_at + by, NY)), by) for by in range(1, NY)]

    far_in = lax.ppermute(inputs[:, 0], "head", z_swap)
    far_grad = lax.ppermute(out_grad[:, 0], "head", z_swap)
    in_parts = head_gather(inputs[:, 0], far_in)
    projected = jnp.einsum(
        "vd,dch->cvh", jnp.concatenate(in_parts, axis=1), qkv_weight, preferred_element_type=F32
    ).astype(BF16)
    far_grad, projected = lax.optimization_barrier((far_grad, projected))
    grad_parts = head_gather(out_grad[:, 0], far_grad)
    grad_attn = jnp.dot(
        jnp.concatenate(grad_parts, axis=1), out_weight, preferred_element_type=F32
    ).astype(BF16)

    kv_all = around(projected[1:])
    qg_all = spread(jnp.stack([projected[0], grad_attn]))

    text_own = text // (NY * NZX)
    text_per = NY * text_own
    slot = lax.broadcasted_iota(jnp.int32, (text_per, text), 0)
    source = lax.broadcasted_iota(jnp.int32, (text_per, text), 1)
    wanted = (lax.rem(y_at + NY - slot // text_own, NY) * NZX + zx) * text_own + lax.rem(
        slot, text_own
    )
    chosen = source == wanted
    select = chosen.astype(BF16)
    tk = jnp.dot(select, text_keys[:, 0], preferred_element_type=F32).astype(BF16)
    tv = jnp.dot(select, text_values[:, 0], preferred_element_type=F32).astype(BF16)
    mask = jnp.sum(jnp.where(chosen, text_mask[:, 0][None, :], 0), axis=1, keepdims=True)
    mask = jnp.broadcast_to(mask, (text_per, HD))

    q_rows = NZX * rows
    grid = (heads,)
    params = pltpu.CompilerParams(
        vmem_limit_bytes=56 * 1024 * 1024, dimension_semantics=("arbitrary",)
    )
    in_specs = (
        [
            pl.BlockSpec((NZX, 1, rows, HD), lambda h: (0, 0, 0, h)),
            pl.BlockSpec((NZX, 1, rows, HD), lambda h: (0, 1, 0, h)),
        ]
        + [pl.BlockSpec((1, rows, HD), lambda h: (0, 0, h))] * NY
        + [pl.BlockSpec((1, rows, HD), lambda h: (1, 0, h))] * NY
        + [
            pl.BlockSpec((text_per, HD), lambda h: (0, h)),
            pl.BlockSpec((text_per, HD), lambda h: (0, h)),
            pl.BlockSpec((text_per, HD), lambda h: (0, 0)),
        ]
    )
    x_in = slices_around(in_parts)
    kv_all, grad_parts = lax.optimization_barrier((kv_all, grad_parts))
    x_grad = slices_around(grad_parts)
    operands = (qg_all, qg_all, *kv_all, *kv_all, tk, tv, mask)
    stats, out_terms = pl.pallas_call(
        stats_kernel,
        grid=grid,
        in_specs=in_specs,
        out_specs=[
            pl.BlockSpec((1, 2, q_rows), lambda h: (h, 0, 0)),
            pl.BlockSpec((NZX, rows, HD), lambda h: (0, 0, h)),
        ],
        out_shape=[
            jax.ShapeDtypeStruct((heads, 2, q_rows), F32),
            jax.ShapeDtypeStruct((NZX, rows, width), BF16),
        ],
        compiler_params=params,
        name="attention_stats",
    )(*operands)
    stats, x_in, x_grad = lax.optimization_barrier((stats, x_in, x_grad))
    all_stats = spread(stats)
    out_all = exchange(out_terms)
    own_stats = lax.dynamic_slice_in_dim(all_stats, zx * rows, rows, 3)
    attn_out = pl.pallas_call(
        combine_kernel,
        grid=(heads,),
        in_specs=[
            pl.BlockSpec((NZX, rows, HD), lambda h: (0, 0, h)),
            pl.BlockSpec((NZX, 1, 2, rows), lambda h: (0, h, 0, 0)),
        ],
        out_specs=pl.BlockSpec((rows, HD), lambda h: (0, h)),
        out_shape=jax.ShapeDtypeStruct((rows, width), BF16),
        compiler_params=pltpu.CompilerParams(vmem_limit_bytes=56 * 1024 * 1024),
        name="combine_out",
    )(out_all, own_stats)

    kv_rows = 2 * rows + 2 * text_own
    dq_terms, *kv_terms = pl.pallas_call(
        grads_kernel,
        grid=grid,
        in_specs=in_specs + [pl.BlockSpec((NZX, 1, 2, q_rows), lambda h: (0, h, 0, 0))],
        out_specs=[pl.BlockSpec((NZX, rows, HD), lambda h: (0, 0, h))]
        + [pl.BlockSpec((kv_rows, HD), lambda h: (0, h))] * NY,
        out_shape=[jax.ShapeDtypeStruct((NZX, rows, width), BF16)]
        + [jax.ShapeDtypeStruct((kv_rows, width), BF16)] * NY,
        compiler_params=params,
        name="attention_grads",
    )(*operands, all_stats)

    kv_sum = kv_terms[0].astype(F32)
    for by in range(1, NY):
        kv_sum += shift(kv_terms[by], NY - by).astype(F32)
    dq_all = exchange(dq_terms)
    kv = kv_sum[: 2 * rows].astype(BF16).reshape(2, rows, width)
    text_sum = kv_sum[2 * rows :].reshape(2, text_own, 1, width)

    own = part // NZX

    def weight_terms(xs, gs):
        count = gs[0].shape[0]
        return pl.pallas_call(
            weights_kernel,
            grid=(2,),
            in_specs=[pl.BlockSpec((rows, part // 2), lambda i: (0, i))] * NY
            + [pl.BlockSpec((count, rows, width), lambda i: (0, 0, 0))] * NY,
            out_specs=pl.BlockSpec((NZX // 2, count, own, width), lambda i: (i, 0, 0, 0)),
            out_shape=jax.ShapeDtypeStruct((NZX, count, own, width), BF16),
            compiler_params=pltpu.CompilerParams(vmem_limit_bytes=56 * 1024 * 1024),
            name="weight_grads",
        )(*xs, *gs)
    def total(array):
        return jnp.sum(array.astype(F32), axis=0)

    outs, kv = lax.optimization_barrier((around(attn_out[None]), kv))
    out_weights = weight_terms(x_grad, outs)
    kvs = around(kv)
    out_weights, first = lax.optimization_barrier((out_weights, kvs[1]))
    kvs = [kvs[0], first] + kvs[2:]
    out_received = exchange(out_weights)
    dq_all, kv = lax.optimization_barrier((dq_all, kv))
    dq = jnp.sum(dq_all.astype(F32), axis=0).astype(BF16)
    grad_projected = jnp.concatenate([dq[None], kv])
    terms = jnp.einsum(
        "cvh,sdch->svd",
        grad_projected,
        qkv_weight.reshape(4, part, 3, width),
        preferred_element_type=F32,
    ).astype(BF16)
    kvs, out_weights, terms = lax.optimization_barrier((kvs, out_weights, terms))
    kv_weights = weight_terms(x_in, kvs)
    kv_weights, out_received = lax.optimization_barrier((kv_weights, out_received))
    kv_received = exchange(kv_weights)

    dqs, kv_weights = lax.optimization_barrier((around(dq[None]), kv_weights))
    q_weights = weight_terms(x_in, dqs)
    q_weights, kv_received = lax.optimization_barrier((q_weights, kv_received))
    qkv_sum = jnp.concatenate([total(exchange(q_weights)), total(kv_received)])
    keep = [jnp.where(core == 0, terms[2 * z], terms[2 * z + 1]) for z in range(2)]
    give = [jnp.where(core == 0, terms[2 * z + 1], terms[2 * z]) for z in range(2)]
    pair = [
        keep[z].astype(F32) + lax.ppermute(give[z], "head", core_swap).astype(F32)
        for z in range(2)
    ]
    mine = jnp.where(z_hi == 0, pair[0], pair[1])
    other = jnp.where(z_hi == 0, pair[1], pair[0]).astype(BF16)
    grad_inputs = (mine + lax.ppermute(other, "head", z_swap).astype(F32)).astype(BF16)

    return (
        grad_inputs[:, None],
        jnp.transpose(qkv_sum, (1, 0, 2)),
        total(out_received)[0],
        text_sum[0],
        text_sum[1],
    )


def solution(mesh):
    return jax.shard_map(
        per_device,
        mesh=mesh,
        in_specs=(
            P("blk", None, "head"),
            P("blk", None, "head"),
            P(None, None, "head"),
            P(None, "head"),
            P(None, None, "head"),
            P(None, None, "head"),
            P(),
        ),
        out_specs=(
            P("blk", None, "head"),
            P("blk", None, "head"),
            P("blk", "head"),
            P("blk", None, "head"),
            P("blk", None, "head"),
        ),
        check_vma=False,
    )
```

```python
import jax
import jax.numpy as jnp
from jax import lax
from jax.experimental import pallas as pl
from jax.experimental.pallas import tpu as pltpu
from jax.sharding import PartitionSpec as P

HD = 128
LOG2E = 1.4426950408889634
MASKED = -1000000000.0 * LOG2E
F32 = jnp.float32
BF16 = jnp.bfloat16
NY = 4
NZX = 8


def nt_dot(a, b):
    return lax.dot_general(a, b, (((1,), (1,)), ((), ())), preferred_element_type=F32)


def nn_dot(a, b):
    return lax.dot_general(a, b, (((1,), (0,)), ((), ())), preferred_element_type=F32)


def tn_dot(a, b):
    return lax.dot_general(a, b, (((0,), (0,)), ((), ())), preferred_element_type=F32)


def rows_of(ref):
    block = ref[...]
    return block.reshape(-1, block.shape[-1])


def pick(parts, value):
    return jnp.concatenate([rows_of(part) for part in parts] + [value], axis=0)


def scores(keys, q, valid, video):
    s = nt_dot(keys, q) * (HD**-0.5 * LOG2E)
    return jnp.concatenate([s[:video], jnp.where(valid, s[video:], MASKED)], axis=0)


def stats_kernel(q_ref, g_ref, *refs):
    ks, vs = refs[:NY], refs[NY : 2 * NY]
    tk_ref, tv_ref, mask_ref, stat_ref, out_ref = refs[2 * NY :]
    q, g = rows_of(q_ref), rows_of(g_ref)
    k, v = pick(ks, tk_ref[...]), pick(vs, tv_ref[...])
    s = scores(k, q, mask_ref[:, 0:1] == 1, k.shape[0] - tk_ref.shape[0])
    top = jnp.max(s, axis=0, keepdims=True)
    p = jnp.exp2(s - top)
    total = jnp.sum(p, axis=0, keepdims=True)
    stat_ref[0, 0:1, :] = top + jnp.log2(total)
    stat_ref[0, 1:2, :] = jnp.sum(p * nt_dot(v, g), axis=0, keepdims=True) / total
    out = tn_dot(v, p.astype(BF16)) / total
    out_ref[...] = out.T.astype(BF16).reshape(out_ref.shape)


def merged(stat_ref):
    logs = [stat_ref[i, 0, 0:1, :] for i in range(NZX)]
    top = logs[0]
    for other in logs[1:]:
        top = jnp.maximum(top, other)
    shares = [jnp.exp2(log - top) for log in logs]
    total = sum(shares[1:], shares[0])
    dot = shares[0] * stat_ref[0, 0, 1:2, :]
    for i in range(1, NZX):
        dot += shares[i] * stat_ref[i, 0, 1:2, :]
    return top + jnp.log2(total), dot / total, shares, total


def combine_kernel(out_ref, stat_ref, o_ref):
    _, _, shares, total = merged(stat_ref)
    rows = out_ref.shape[1]
    acc = jnp.zeros((rows, HD), F32)
    for i in range(NZX):
        weight = jnp.broadcast_to(shares[i] / total, (HD, rows)).T
        acc += weight * out_ref[i].astype(F32)
    o_ref[...] = acc.astype(BF16)


def grads_kernel(q_ref, g_ref, *refs):
    ks, vs = refs[:NY], refs[NY : 2 * NY]
    tk_ref, tv_ref, mask_ref, stat_ref, dq_ref = refs[2 * NY : 2 * NY + 5]
    kv_refs = refs[2 * NY + 5 :]
    q, g = rows_of(q_ref), rows_of(g_ref)
    k, v = pick(ks, tk_ref[...]), pick(vs, tv_ref[...])
    keys = k.shape[0] - tk_ref.shape[0]
    log_total, dot, _, _ = merged(stat_ref)
    s = scores(k, q, mask_ref[:, 0:1] == 1, keys)
    p = jnp.exp2(s - log_total)
    ds = (p * (nt_dot(v, g) - dot)).astype(BF16)
    dq = tn_dot(k, ds) * HD**-0.5
    dq_ref[...] = dq.T.astype(BF16).reshape(dq_ref.shape)

    dk = nn_dot(ds, q) * HD**-0.5
    dv = nn_dot(p.astype(BF16), g)
    per = keys // NY
    text = (dk.shape[0] - keys) // NY
    for y in range(NY):
        own, at = slice(y * per, (y + 1) * per), slice(keys + y * text, keys + (y + 1) * text)
        kv_refs[y][:per] = dk[own].astype(BF16)
        kv_refs[y][per : 2 * per] = dv[own].astype(BF16)
        kv_refs[y][2 * per :] = jnp.concatenate([dk[at], dv[at]], axis=0).astype(BF16)


def weights_kernel(*refs):
    xs, gs, o_ref = refs[:NY], refs[NY:-1], refs[-1]
    acc = None
    for y in range(NY):
        g = [gs[y][c] for c in range(gs[y].shape[0])]
        term = tn_dot(xs[y][...], g[0] if len(g) == 1 else jnp.concatenate(g, axis=1))
        acc = term if acc is None else acc + term
    width = o_ref.shape[3]
    for c in range(o_ref.shape[1]):
        part = acc[:, c * width : (c + 1) * width].astype(BF16)
        o_ref[:, c] = part.reshape(o_ref.shape[0], o_ref.shape[2], width)


def per_device(inputs, out_grad, qkv_weight, out_weight, text_keys, text_values, text_mask):
    rows = inputs.shape[0]
    part = inputs.shape[2]
    width = qkv_weight.shape[2]
    heads = width // HD
    text = text_keys.shape[0]
    blk = lax.axis_index("blk")
    head = lax.axis_index("head")
    zx, y_at = lax.rem(blk, NZX), blk // NZX
    core, z_hi = lax.rem(head, 2), head // 2
    along_zx = [[y * NZX + i for i in range(NZX)] for y in range(NY)]
    core_swap = [(i, i ^ 1) for i in range(4)]
    z_swap = [(i, i ^ 2) for i in range(4)]

    def exchange(array):
        return lax.all_to_all(array, "blk", 0, 0, tiled=True, axis_index_groups=along_zx)

    def spread(array):
        return exchange(jnp.broadcast_to(array[None], (NZX,) + array.shape))

    def shift(array, by):
        return lax.ppermute(
            array, "blk", [(i, (i + by * NZX) % (NY * NZX)) for i in range(NY * NZX)]
        )

    def around(array):
        return [array] + [shift(array, by) for by in range(1, NY)]

    def head_gather(own, far):
        near = lax.ppermute(own, "head", core_swap)
        far_near = lax.ppermute(far, "head", core_swap)
        return [
            jnp.where(
                z_hi == z,
                jnp.where(core == c, own, near),
                jnp.where(core == c, far, far_near),
            )
            for z in range(2)
            for c in range(2)
        ]

    def slices_around(parts):
        def slice_for(y):
            return jnp.where(
                y < 2, jnp.where(y == 0, parts[0], parts[1]), jnp.where(y == 2, parts[2], parts[3])
            )

        own = slice_for(y_at)
        return [own] + [shift(slice_for(lax.rem(y_at + by, NY)), by) for by in range(1, NY)]

    far_in = lax.ppermute(inputs[:, 0], "head", z_swap)
    far_grad = lax.ppermute(out_grad[:, 0], "head", z_swap)
    in_parts = head_gather(inputs[:, 0], far_in)
    projected = jnp.einsum(
        "vd,dch->cvh", jnp.concatenate(in_parts, axis=1), qkv_weight, preferred_element_type=F32
    ).astype(BF16)
    far_grad, projected = lax.optimization_barrier((far_grad, projected))
    grad_parts = head_gather(out_grad[:, 0], far_grad)
    grad_attn = jnp.dot(
        jnp.concatenate(grad_parts, axis=1), out_weight, preferred_element_type=F32
    ).astype(BF16)

    kv_all = around(projected[1:])
    qg_all = spread(jnp.stack([projected[0], grad_attn]))

    text_own = text // (NY * NZX)
    text_per = NY * text_own
    slot = lax.broadcasted_iota(jnp.int32, (text_per, text), 0)
    source = lax.broadcasted_iota(jnp.int32, (text_per, text), 1)
    wanted = (lax.rem(y_at + NY - slot // text_own, NY) * NZX + zx) * text_own + lax.rem(
        slot, text_own
    )
    chosen = source == wanted
    select = chosen.astype(BF16)
    tk = jnp.dot(select, text_keys[:, 0], preferred_element_type=F32).astype(BF16)
    tv = jnp.dot(select, text_values[:, 0], preferred_element_type=F32).astype(BF16)
    mask = jnp.sum(jnp.where(chosen, text_mask[:, 0][None, :], 0), axis=1, keepdims=True)
    mask = jnp.broadcast_to(mask, (text_per, HD))

    q_rows = NZX * rows
    grid = (heads,)
    params = pltpu.CompilerParams(
        vmem_limit_bytes=56 * 1024 * 1024, dimension_semantics=("arbitrary",)
    )
    in_specs = (
        [
            pl.BlockSpec((NZX, 1, rows, HD), lambda h: (0, 0, 0, h)),
            pl.BlockSpec((NZX, 1, rows, HD), lambda h: (0, 1, 0, h)),
        ]
        + [pl.BlockSpec((1, rows, HD), lambda h: (0, 0, h))] * NY
        + [pl.BlockSpec((1, rows, HD), lambda h: (1, 0, h))] * NY
        + [
            pl.BlockSpec((text_per, HD), lambda h: (0, h)),
            pl.BlockSpec((text_per, HD), lambda h: (0, h)),
            pl.BlockSpec((text_per, HD), lambda h: (0, 0)),
        ]
    )
    x_in = slices_around(in_parts)
    kv_all, grad_parts = lax.optimization_barrier((kv_all, grad_parts))
    x_grad = slices_around(grad_parts)
    operands = (qg_all, qg_all, *kv_all, *kv_all, tk, tv, mask)
    stats, out_terms = pl.pallas_call(
        stats_kernel,
        grid=grid,
        in_specs=in_specs,
        out_specs=[
            pl.BlockSpec((1, 2, q_rows), lambda h: (h, 0, 0)),
            pl.BlockSpec((NZX, rows, HD), lambda h: (0, 0, h)),
        ],
        out_shape=[
            jax.ShapeDtypeStruct((heads, 2, q_rows), F32),
            jax.ShapeDtypeStruct((NZX, rows, width), BF16),
        ],
        compiler_params=params,
        name="attention_stats",
    )(*operands)
    stats, x_in, x_grad = lax.optimization_barrier((stats, x_in, x_grad))
    all_stats = spread(stats)
    out_all = exchange(out_terms)
    own_stats = lax.dynamic_slice_in_dim(all_stats, zx * rows, rows, 3)
    attn_out = pl.pallas_call(
        combine_kernel,
        grid=(heads,),
        in_specs=[
            pl.BlockSpec((NZX, rows, HD), lambda h: (0, 0, h)),
            pl.BlockSpec((NZX, 1, 2, rows), lambda h: (0, h, 0, 0)),
        ],
        out_specs=pl.BlockSpec((rows, HD), lambda h: (0, h)),
        out_shape=jax.ShapeDtypeStruct((rows, width), BF16),
        compiler_params=pltpu.CompilerParams(vmem_limit_bytes=56 * 1024 * 1024),
        name="combine_out",
    )(out_all, own_stats)

    kv_rows = 2 * rows + 2 * text_own
    dq_terms, *kv_terms = pl.pallas_call(
        grads_kernel,
        grid=grid,
        in_specs=in_specs + [pl.BlockSpec((NZX, 1, 2, q_rows), lambda h: (0, h, 0, 0))],
        out_specs=[pl.BlockSpec((NZX, rows, HD), lambda h: (0, 0, h))]
        + [pl.BlockSpec((kv_rows, HD), lambda h: (0, h))] * NY,
        out_shape=[jax.ShapeDtypeStruct((NZX, rows, width), BF16)]
        + [jax.ShapeDtypeStruct((kv_rows, width), BF16)] * NY,
        compiler_params=params,
        name="attention_grads",
    )(*operands, all_stats)

    kv_sum = kv_terms[0].astype(F32)
    for by in range(1, NY):
        kv_sum += shift(kv_terms[by], NY - by).astype(F32)
    dq_all = exchange(dq_terms)
    kv = kv_sum[: 2 * rows].astype(BF16).reshape(2, rows, width)
    text_sum = kv_sum[2 * rows :].reshape(2, text_own, 1, width)

    own = part // NZX

    def weight_terms(xs, gs):
        count = gs[0].shape[0]
        return pl.pallas_call(
            weights_kernel,
            grid=(1,),
            in_specs=[pl.BlockSpec((rows, part), lambda i: (0, i))] * NY
            + [pl.BlockSpec((count, rows, width), lambda i: (0, 0, 0))] * NY,
            out_specs=pl.BlockSpec((NZX, count, own, width), lambda i: (i, 0, 0, 0)),
            out_shape=jax.ShapeDtypeStruct((NZX, count, own, width), BF16),
            compiler_params=pltpu.CompilerParams(vmem_limit_bytes=56 * 1024 * 1024),
            name="weight_grads",
        )(*xs, *gs)
    def total(array):
        return jnp.sum(array.astype(F32), axis=0)

    outs, kv = lax.optimization_barrier((around(attn_out[None]), kv))
    out_weights = weight_terms(x_grad, outs)
    kvs = around(kv)
    out_weights, first = lax.optimization_barrier((out_weights, kvs[1]))
    kvs = [kvs[0], first] + kvs[2:]
    out_received = exchange(out_weights)
    dq_all, kv = lax.optimization_barrier((dq_all, kv))
    dq = jnp.sum(dq_all.astype(F32), axis=0).astype(BF16)
    grad_projected = jnp.concatenate([dq[None], kv])
    terms = jnp.einsum(
        "cvh,sdch->svd",
        grad_projected,
        qkv_weight.reshape(4, part, 3, width),
        preferred_element_type=F32,
    ).astype(BF16)
    kvs, out_weights, terms = lax.optimization_barrier((kvs, out_weights, terms))
    kv_weights = weight_terms(x_in, kvs)
    kv_weights, out_received = lax.optimization_barrier((kv_weights, out_received))
    kv_received = exchange(kv_weights)

    dqs, kv_weights = lax.optimization_barrier((around(dq[None]), kv_weights))
    q_weights = weight_terms(x_in, dqs)
    q_weights, kv_received = lax.optimization_barrier((q_weights, kv_received))
    qkv_sum = jnp.concatenate([total(exchange(q_weights)), total(kv_received)])
    keep = [jnp.where(core == 0, terms[2 * z], terms[2 * z + 1]) for z in range(2)]
    give = [jnp.where(core == 0, terms[2 * z + 1], terms[2 * z]) for z in range(2)]
    pair = [
        keep[z].astype(F32) + lax.ppermute(give[z], "head", core_swap).astype(F32)
        for z in range(2)
    ]
    mine = jnp.where(z_hi == 0, pair[0], pair[1])
    other = jnp.where(z_hi == 0, pair[1], pair[0]).astype(BF16)
    grad_inputs = (mine + lax.ppermute(other, "head", z_swap).astype(F32)).astype(BF16)

    return (
        grad_inputs[:, None],
        jnp.transpose(qkv_sum, (1, 0, 2)),
        total(out_received)[0],
        text_sum[0],
        text_sum[1],
    )


def solution(mesh):
    return jax.shard_map(
        per_device,
        mesh=mesh,
        in_specs=(
            P("blk", None, "head"),
            P("blk", None, "head"),
            P(None, None, "head"),
            P(None, "head"),
            P(None, None, "head"),
            P(None, None, "head"),
            P(),
        ),
        out_specs=(
            P("blk", None, "head"),
            P("blk", None, "head"),
            P("blk", "head"),
            P("blk", None, "head"),
            P("blk", None, "head"),
        ),
        check_vma=False,
    )
```
